32 devices in a mesh: dp: 8 (over y, x, core), tensor: 4 (over z).
Axes of the slice: x: 2, y: 2, z: 4, core: 2. Of those that a mesh axis runs over, the one named last changes fastest.
Arguments:
- tokens: bfloat16 [4096, 768], P(('dp', 'tensor')), may hold values from -2.5 to 2.5
- condition: bfloat16 [8, 768], P('dp'), may hold values from -2.5 to 2.5
- modulate_weight: bfloat16 [768, 4608], P(None, 'tensor'), may hold values from -0.21875 to 0.21875
- modulate_bias: float32 [4608], P('tensor'), may hold values from -0.75 to 0.75
- heads_weight: bfloat16 [3, 768, 768], P(None, None, 'tensor'), may hold values from -0.21875 to 0.21875
- heads_bias: float32 [2, 768], P(None, 'tensor'), may hold values from -0.75 to 0.75
- output_weight: bfloat16 [768, 768], P('tensor'), may hold values from -0.875 to 0.875
- output_bias: float32 [768], replicated, may hold values from -0.75 to 0.75
- first_weight: bfloat16 [768, 3072], P(None, 'tensor'), may hold values from -0.21875 to 0.21875
- first_bias: float32 [3072], P('tensor'), may hold values from -0.75 to 0.75
- second_weight: bfloat16 [3072, 768], P('tensor'), may hold values from -0.109375 to 0.109375
- second_bias: float32 [768], replicated, may hold values from -0.75 to 0.75
- cotangent: bfloat16 [4096, 768], P(('dp', 'tensor')), may hold values from -2.5 to 2.5
Outputs:
- output: bfloat16 [4096, 768], P(('dp', 'tensor'))
- token_grad: float32 [4096, 768], P(('dp', 'tensor'))
- modulate_weight_grad: float32 [768, 4608], P('dp', 'tensor')
- modulate_bias_grad: float32 [4608], P('tensor')
- heads_weight_grad: float32 [3, 768, 768], P(None, 'dp', 'tensor')
- heads_bias_grad: float32 [2, 768], P(None, 'tensor')
- output_weight_grad: float32 [768, 768], P('tensor', 'dp')
- output_bias_grad: float32 [768], replicated
- first_weight_grad: float32 [768, 3072], P('dp', 'tensor')
- first_bias_grad: float32 [3072], P('tensor')
- second_weight_grad: float32 [3072, 768], P('tensor', 'dp')
- second_bias_grad: float32 [768], replicated
The draws below stay inside these ranges and needn't reach their ends.
All inputs are finite; a program needn't handle non-finite values.
Results may differ from the reference program's by a relative error of at most 0.012.
The reference program's roundings to bfloat16 on the way count: a program that leaves them out, or rounds other values in their place, can miss the bound.
Values may be sent and summed in bfloat16 or wider, within the bound.
A program may use at most 128 MiB of HBM per device.

```python
import jax
import jax.numpy as jnp
from jax import lax

H = 12
HD = 64
FF = 3072
D = 768
LEN = 512
LAT = 8
TOKENS = 4096


def steps_of(stream_key, extent, cuts, least, largest):
    def one(position, shards_of):
        steps = jax.random.uniform(jax.random.fold_in(jax.random.fold_in(stream_key, 6), position), (shards_of,), jnp.float32, least / len(cuts), largest / len(cuts))
        return jnp.repeat(jnp.exp(steps), extent[position] // shards_of).reshape((-1,) + (1,) * (len(extent) - position - 1))

    level = one(*cuts[0])
    for cut in cuts[1:]:
        level = level * one(*cut)
    return level


def gaussian(rng, shape, deviation, bound, cuts=(), dtype=jnp.bfloat16):
    factor_of = steps_of(rng, shape, cuts, -0.22, 0.18) if cuts else 1.0
    values = jax.random.normal(rng, shape, jnp.float32) * deviation * factor_of
    return jnp.minimum(jnp.maximum(values, -bound), bound).astype(dtype)


def setup_inputs(seed: int = 0) -> dict:
    key_list = jax.random.split(jax.random.key(seed), 14)
    return {
        "tokens": gaussian(key_list[0], (TOKENS, D), 1.0, 2.5, ((0, 32),)),
        "condition": gaussian(key_list[1], (LAT, D), 1.0, 2.5, ((0, 8),)),
        "modulate_weight": gaussian(key_list[2], (D, 6 * D), D ** -0.5, 0.21875, ((1, 4),)),
        "modulate_bias": gaussian(key_list[3], (6 * D,), 0.3, 0.75, ((0, 4),), jnp.float32),
        "heads_weight": gaussian(key_list[4], (3, D, D), D ** -0.5, 0.21875, ((2, 4),)),
        "heads_bias": gaussian(key_list[5], (2, D), 0.3, 0.75, ((1, 4),), jnp.float32),
        "output_weight": gaussian(key_list[6], (D, D), (D // 16) ** -0.5, 0.875, ((0, 4),)),
        "output_bias": gaussian(key_list[7], (D,), 0.3, 0.75, (), jnp.float32),
        "first_weight": gaussian(key_list[8], (D, FF), D ** -0.5, 0.21875, ((1, 4),)),
        "first_bias": gaussian(key_list[9], (FF,), 0.3, 0.75, ((0, 4),), jnp.float32),
        "second_weight": gaussian(key_list[10], (FF, D), FF ** -0.5, 0.109375, ((0, 4),)),
        "second_bias": gaussian(key_list[11], (D,), 0.3, 0.75, (), jnp.float32),
        "cotangent": gaussian(key_list[12], (TOKENS, D), 1.0, 2.5, ((0, 32),)),
    }


EPSILON = 1e-06
HIGHEST_PRECISION = lax.Precision.HIGHEST

@jax.custom_vjp
def low(v):
    return lax.optimization_barrier(v.astype(jnp.bfloat16)).astype(jnp.float32)

@jax.custom_vjp
def low_back(v):
    return v

def low_keep(v):
    return (low(v), None)

def low_pass(kept, grad):
    return (grad,)

def back_keep(v):
    return (v, None)

def back_low(kept, grad):
    return (low(grad),)
low.defvjp(low_keep, low_pass)
low_back.defvjp(back_keep, back_low)

def dense(left, right):
    return jnp.dot(left, right, precision=HIGHEST_PRECISION, preferred_element_type=jnp.float32)

def layer_norm(values):
    centred = values - lax.optimization_barrier(jnp.mean(values, axis=-1, keepdims=True))
    spread = lax.optimization_barrier(jnp.mean(centred * centred, axis=-1, keepdims=True))
    return centred * lax.rsqrt(spread + EPSILON)

def attend_latent(queries, key_rows, value_rows):
    query_heads = queries.reshape(LEN, H, HD)
    key_heads = key_rows.reshape(LEN, H, HD)
    value_heads = value_rows.reshape(LEN, H, HD)
    scores = jnp.einsum('qhd,khd->hqk', query_heads, key_heads, precision=HIGHEST_PRECISION) * HD ** (-0.5)
    scores = low_back(scores)
    probability = low(jax.nn.softmax(scores, axis=-1))
    mixture = jnp.einsum('hqk,khd->qhd', probability, value_heads, precision=HIGHEST_PRECISION)
    return mixture.reshape(LEN, H * HD)

def attend_blocks(blocks):
    return jax.checkpoint(attend_latent)(blocks[0], blocks[1], blocks[2])

def block_forward(token_rows, cond_rows, modulate_weight, modulate_bias, heads_weight, heads_bias, output_weight, output_bias, first_weight, first_bias, second_weight, second_bias):
    model_width = H * HD
    latents = cond_rows.shape[0]
    silu_cond = low(jax.nn.silu(cond_rows))
    modulation = (dense(silu_cond, modulate_weight) + modulate_bias).reshape(latents, 6, model_width)
    pieces = [jnp.repeat(modulation[:, member, :], LEN, axis=0) for member in range(6)]
    shift_a, scale_a, gate_a, shift_f, scale_f, gate_f = pieces
    attention_in = low(layer_norm(token_rows) * (1.0 + scale_a) + shift_a)
    queries = low_back(low(dense(attention_in, heads_weight[0]) + heads_bias[0]))
    key_rows = low_back(low(dense(attention_in, heads_weight[1])))
    value_rows = low_back(low(dense(attention_in, heads_weight[2]) + heads_bias[1]))
    shaped = (latents, LEN, model_width)
    mixture = lax.map(attend_blocks, (queries.reshape(shaped), key_rows.reshape(shaped), value_rows.reshape(shaped)))
    mixture = low_back(low(mixture.reshape(latents * LEN, model_width)))
    branch_a = low_back(dense(mixture, output_weight) + output_bias)
    residual_mid = token_rows + gate_a * branch_a
    feed_in = low(layer_norm(residual_mid) * (1.0 + scale_f) + shift_f)
    hidden_pre = low_back(dense(feed_in, first_weight) + first_bias)
    activated = low(jax.nn.gelu(hidden_pre, approximate=True))
    branch_f = low_back(dense(activated, second_weight) + second_bias)
    return residual_mid + gate_f * branch_f

def reference(tokens, condition, modulate_weight, modulate_bias, heads_weight, heads_bias, output_weight, output_bias, first_weight, first_bias, second_weight, second_bias, cotangent):
    params = tuple((item.astype(jnp.float32) for item in (modulate_weight, modulate_bias, heads_weight, heads_bias, output_weight, output_bias, first_weight, first_bias, second_weight, second_bias)))
    model_width = H * HD
    latents = condition.shape[0]
    group = 1
    for option in range(1, latents + 1):
        if latents % option == 0 and option * LEN <= 4096:
            group = option
    rounds = latents // group
    token_groups = tokens.astype(jnp.float32).reshape(rounds, group * LEN, model_width)
    cond_groups = condition.astype(jnp.float32).reshape(rounds, group, model_width)
    tangent_groups = cotangent.astype(jnp.float32).reshape(rounds, group * LEN, model_width)
    initial = tuple((jnp.zeros_like(item) for item in params))

    def step_group(totals, inputs):
        token_part, cond_part, tangent_part = inputs

        def forward(token_arg, *weights):
            return block_forward(token_arg, cond_part, *weights)
        result, pullback = jax.vjp(forward, token_part, *params)
        grads = pullback(tangent_part)
        totals = tuple((total + grade for total, grade in zip(totals, grads[1:])))
        return (totals, (result.astype(jnp.bfloat16), grads[0]))
    totals, (outputs, token_grads) = lax.scan(step_group, initial, (token_groups, cond_groups, tangent_groups))
    output = outputs.reshape(latents * LEN, model_width)
    token_grad = token_grads.reshape(latents * LEN, model_width)
    return (output, token_grad, totals[0], totals[1], totals[2], totals[3], totals[4], totals[5], totals[6], totals[7], totals[8], totals[9])
```

```python
from functools import partial

import jax
import jax.numpy as jnp
from jax import lax
from jax.experimental import pallas as pl
from jax.experimental.pallas import tpu as pltpu
from jax.sharding import PartitionSpec as P

HD = 64
LEN = 512


EPSILON = 1e-06
HIGHEST_PRECISION = lax.Precision.HIGHEST


def layer_norm(values):
    centred = values - jnp.mean(values, axis=-1, keepdims=True)
    inverse = lax.rsqrt(jnp.mean(centred * centred, axis=-1, keepdims=True) + EPSILON)
    return (centred * inverse, inverse)


def norm_back(grade, normed, inverse):
    return inverse * (
        grade
        - jnp.mean(grade, axis=-1, keepdims=True)
        - normed * jnp.mean(grade * normed, axis=-1, keepdims=True)
    )


def matmul(left, right):
    return jnp.dot(left, right, preferred_element_type=jnp.float32)


def left_contract(left, right):
    return lax.dot_general(
        left, right, (((0,), (0,)), ((), ())), preferred_element_type=jnp.float32
    )


def right_contract(left, right):
    return lax.dot_general(
        left, right, (((1,), (1,)), ((), ())), preferred_element_type=jnp.float32
    )


def exact_left(left, right):
    return lax.dot_general(
        left,
        right,
        (((0,), (0,)), ((), ())),
        precision=HIGHEST_PRECISION,
        preferred_element_type=jnp.float32,
    )


def head_cols(values, head):
    return values[:, head * HD : (head + 1) * HD]


def attend_forward(blocks):
    query_block, key_block, value_block = blocks
    outputs = []
    sums = []
    for head in range(query_block.shape[1] // HD):
        scores = right_contract(head_cols(query_block, head), head_cols(key_block, head)) * HD ** (
            -0.5
        )
        peak = jnp.max(scores, axis=-1, keepdims=True)
        expo = jnp.exp(scores - peak)
        total = jnp.sum(expo, axis=-1, keepdims=True)
        probability = (expo / total).astype(jnp.bfloat16)
        outputs.append(matmul(probability, head_cols(value_block, head)))
        sums.append((peak + jnp.log(total))[:, 0])
    return (jnp.concatenate(outputs, axis=1).astype(jnp.bfloat16), jnp.stack(sums))


def attend_backward(blocks):
    query_block, key_block, value_block, grade_block, logsum = blocks
    query_parts = []
    key_parts = []
    value_parts = []
    for head in range(query_block.shape[1] // HD):
        query_head = head_cols(query_block, head)
        key_head = head_cols(key_block, head)
        grade_head = head_cols(grade_block, head)
        scores = right_contract(query_head, key_head) * HD ** (-0.5)
        probability = jnp.exp(scores - logsum[head][:, None])
        value_parts.append(left_contract(probability.astype(jnp.bfloat16), grade_head))
        prob_grad = right_contract(grade_head, head_cols(value_block, head))
        score_grad = probability * (
            prob_grad - jnp.sum(probability * prob_grad, axis=-1, keepdims=True)
        )
        score_low = score_grad.astype(jnp.bfloat16)
        query_parts.append(matmul(score_low, key_head) * HD ** (-0.5))
        key_parts.append(left_contract(score_low, query_head) * HD ** (-0.5))
    return [
        jnp.concatenate(parts, axis=1).astype(jnp.bfloat16)
        for parts in (query_parts, key_parts, value_parts)
    ]


MESH = pl.DeviceIdType.MESH
PARAMS = dict(has_side_effects=True, vmem_limit_bytes=40 * 1024 * 1024)


def greet(groups):
    barrier = pltpu.get_barrier_semaphore()
    count = 0
    for axis, peers in groups:
        for peer in peers:
            pl.semaphore_signal(barrier, inc=1, device_id={axis: peer}, device_id_type=MESH)
            count += 1
    pl.semaphore_wait(barrier, count)


def remote(src, dst, sems, slot, axis, peer):
    copy = pltpu.make_async_remote_copy(
        src_ref=src,
        dst_ref=dst,
        send_sem=sems.at[0, slot],
        recv_sem=sems.at[1, slot],
        device_id={axis: peer},
        device_id_type=MESH,
    )
    copy.start()
    return copy


def exchange_kernel(n_t, n_d, n_gather, n_reduce, n_dp, *refs):
    refs = list(refs)

    def take(count):
        taken = refs[:count]
        del refs[:count]
        return taken

    gather_in, reduce_in, dp_in = take(n_gather), take(n_reduce), take(n_dp)
    gather_out, reduce_out, dp_out = take(n_gather), take(n_reduce), take(n_dp)
    gather_sems = take(n_gather)
    reduce_scratch = [take(2) for _ in range(n_reduce)]
    dp_scratch = [take(5) for _ in range(n_dp)]
    rank = lax.axis_index("tensor")
    t_peers = [lax.rem(rank + k, n_t) for k in range(1, n_t)]
    groups = [("tensor", t_peers)]
    n_chip = n_d // 2
    if n_dp:
        place = lax.axis_index("dp")
        chip = place // 2
        core = lax.rem(place, 2)
        chips = [lax.rem(chip + k, n_chip) for k in range(n_chip)]
        sibling = chip * 2 + 1 - core
        d_peers = [chips[k] * 2 + core for k in range(1, n_chip)]
        groups.append(("dp", [sibling] + d_peers))
    greet(groups)
    order = list(range(1, n_chip)) + [0]
    pending = []
    first_phase = []
    for src, (near, outgoing, far, near_sems, far_sems) in zip(dp_in, dp_scratch):
        first_phase.append(
            {
                k: remote(src.at[chips[k], 1 - core], near.at[k], near_sems, k, "dp", sibling)
                for k in order
            }
        )
    gathers = []
    for src, dst, sems in zip(gather_in, gather_out, gather_sems):
        rows = src.shape[0]
        own = pl.ds(pl.multiple_of(rank * rows, rows), rows)
        for k, peer in enumerate(t_peers):
            gathers.append(remote(src, dst.at[own], sems, k, "tensor", peer))
    reduces = []
    for src, (landed, sems) in zip(reduce_in, reduce_scratch):
        rows = landed.shape[1]
        copies = []
        for k, peer in enumerate(t_peers):
            part = pl.ds(pl.multiple_of(peer * rows, rows), rows)
            copies.append(remote(src.at[part], landed.at[k], sems, k, "tensor", peer))
        reduces.append(copies)
    second_phase = []
    for src, out, copies, (near, outgoing, far, near_sems, far_sems) in zip(
        dp_in, dp_out, first_phase, dp_scratch
    ):
        later = []
        for k in order:
            copies[k].wait_recv()
            value = src[chips[k], core].astype(jnp.float32) + near[k].astype(jnp.float32)
            if k == 0:
                out[...] = value
            else:
                outgoing[k - 1] = value.astype(outgoing.dtype)
                later.append(
                    remote(
                        outgoing.at[k - 1], far.at[k - 1], far_sems, k - 1, "dp", d_peers[k - 1]
                    )
                )
        second_phase.append(later)
    for src, dst in zip(gather_in, gather_out):
        rows = src.shape[0]
        dst[pl.ds(pl.multiple_of(rank * rows, rows), rows), :] = src[...]
    for src, out, copies, (landed, sems) in zip(reduce_in, reduce_out, reduces, reduce_scratch):
        rows = landed.shape[1]
        total = src[pl.ds(pl.multiple_of(rank * rows, rows), rows), :].astype(jnp.float32)
        for k, copy in enumerate(copies):
            copy.wait_recv()
            total = total + landed[k].astype(jnp.float32)
        out[...] = total
    for copy in gathers:
        copy.wait_recv()
    for out, later, scratch in zip(dp_out, second_phase, dp_scratch):
        total = out[...]
        for k, copy in enumerate(later):
            copy.wait_recv()
            total = total + scratch[2][k].astype(jnp.float32)
        out[...] = total
    for copy in gathers:
        copy.wait_send()
    for copies in reduces + second_phase:
        for copy in copies:
            copy.wait_send()
    for copies in first_phase:
        for k in order:
            copies[k].wait_send()


def exchange(ident, gathers=(), reduces=(), dp_reduces=()):
    n_t, n_d = lax.axis_size("tensor"), lax.axis_size("dp")
    n_chip = n_d // 2
    outs = []
    scratch = []
    by_kernel = n_d <= 8 and n_d % 2 == 0
    inputs = list(gathers) + list(reduces)
    for value in gathers:
        outs.append(jax.ShapeDtypeStruct((n_t * value.shape[0], value.shape[1]), value.dtype))
        scratch.append(pltpu.SemaphoreType.DMA((2, n_t - 1)))
    for value in reduces:
        rows, columns = value.shape[0] // n_t, value.shape[1]
        outs.append(jax.ShapeDtypeStruct((rows, columns), jnp.float32))
        scratch.append(pltpu.VMEM((n_t - 1, rows, columns), value.dtype))
        scratch.append(pltpu.SemaphoreType.DMA((2, n_t - 1)))
    n_dp = 0
    if by_kernel:
        for value in dp_reduces:
            rows, columns = value.shape[0] // n_d, value.shape[1]
            n_dp += 1
            inputs.append(value.reshape(n_chip, 2, rows, columns))
            outs.append(jax.ShapeDtypeStruct((rows, columns), jnp.float32))
            scratch += [
                pltpu.VMEM((n_chip, rows, columns), value.dtype),
                pltpu.VMEM((n_chip - 1, rows, columns), value.dtype),
                pltpu.VMEM((n_chip - 1, rows, columns), value.dtype),
                pltpu.SemaphoreType.DMA((2, n_chip)),
                pltpu.SemaphoreType.DMA((2, n_chip - 1)),
            ]
    results = pl.pallas_call(
        partial(exchange_kernel, n_t, n_d, len(gathers), len(reduces), n_dp),
        out_shape=outs,
        in_specs=[pl.BlockSpec(memory_space=pltpu.VMEM)] * len(inputs),
        out_specs=[pl.BlockSpec(memory_space=pltpu.VMEM)] * len(outs),
        scratch_shapes=scratch,
        compiler_params=pltpu.CompilerParams(collective_id=ident, **PARAMS),
        name="exchange_%d" % ident,
    )(*inputs)
    if not by_kernel:
        results = list(results) + [
            lax.psum_scatter(value.astype(jnp.float32), "dp", scatter_dimension=0, tiled=True)
            for value in dp_reduces
        ]
    return results


def vector_kernel(n_t, n_d, first, shares, first_all, share_all, landed, total, *sems):
    first_sems, part_sems, total_sems = sems
    rank, place = lax.axis_index("tensor"), lax.axis_index("dp")
    t_peers = [lax.rem(rank + k, n_t) for k in range(1, n_t)]
    d_peers = [lax.rem(place + k, n_d) for k in range(1, n_d)]
    greet([("tensor", t_peers), ("dp", d_peers)])
    parts = [
        remote(shares.at[peer], landed.at[k], part_sems, k, "tensor", peer)
        for k, peer in enumerate(t_peers)
    ]
    copies = [
        remote(first, first_all.at[place], first_sems, k, "dp", peer)
        for k, peer in enumerate(d_peers)
    ]
    value = shares[rank]
    for k, copy in enumerate(parts):
        copy.wait_recv()
        value = value + landed[k]
    total[...] = value
    copies += [
        remote(total, share_all.at[place], total_sems, k, "dp", peer)
        for k, peer in enumerate(d_peers)
    ]
    share_all[place] = value
    first_all[place] = first[...]
    for copy in copies:
        copy.wait_recv()
    for copy in copies + parts:
        copy.wait_send()


def gather_vectors(ident, first, shares):
    n_t, n_d = lax.axis_size("tensor"), lax.axis_size("dp")
    if n_d > 8:
        total = lax.psum_scatter(shares, "tensor", scatter_dimension=0, tiled=True)
        return (lax.all_gather(first, "dp"), lax.all_gather(total, "dp"))
    length, width = first.shape[0], shares.shape[0] // n_t
    length_rows, width_rows = -(-length // 1024) * 8, -(-width // 1024) * 8
    first = jnp.pad(first, (0, length_rows * 128 - length)).reshape(length_rows, 128)
    shares = jnp.pad(shares.reshape(n_t, width), ((0, 0), (0, width_rows * 128 - width)))
    shares = shares.reshape(n_t, width_rows, 128)
    first_all, share_all = pl.pallas_call(
        partial(vector_kernel, n_t, n_d),
        out_shape=[
            jax.ShapeDtypeStruct((n_d, length_rows, 128), jnp.float32),
            jax.ShapeDtypeStruct((n_d, width_rows, 128), jnp.float32),
        ],
        in_specs=[pl.BlockSpec(memory_space=pltpu.VMEM)] * 2,
        out_specs=[pl.BlockSpec(memory_space=pltpu.VMEM)] * 2,
        scratch_shapes=[
            pltpu.VMEM((n_t - 1, width_rows, 128), jnp.float32),
            pltpu.VMEM((width_rows, 128), jnp.float32),
            pltpu.SemaphoreType.DMA((2, n_d - 1)),
            pltpu.SemaphoreType.DMA((2, n_t - 1)),
            pltpu.SemaphoreType.DMA((2, n_d - 1)),
        ],
        compiler_params=pltpu.CompilerParams(collective_id=ident, **PARAMS),
        name="gather_vectors",
    )(first, shares)
    return (
        first_all.reshape(n_d, -1)[:, :length],
        share_all.reshape(n_d, -1)[:, :width],
    )


def local(
    tokens,
    condition,
    modulate_weight,
    modulate_bias,
    heads_weight,
    heads_bias,
    output_weight,
    output_bias,
    first_weight,
    first_bias,
    second_weight,
    second_bias,
    cotangent,
):
    row_count, model_width = tokens.shape
    n_t, n_d = lax.axis_size("tensor"), lax.axis_size("dp")
    local_width = heads_weight.shape[2]
    assert condition.shape[0] == 1 and n_t * row_count == LEN
    low = jnp.bfloat16
    silu_cond = jax.nn.silu(condition.astype(jnp.float32)).astype(low)
    modulate_local = matmul(silu_cond, modulate_weight) + modulate_bias
    mod_width = modulate_local.shape[1]
    mod_rows = -(-mod_width // 1024) * 8
    padded = jnp.pad(modulate_local[0], (0, mod_rows * 128 - mod_width)).reshape(mod_rows, 128)
    (modulation,) = exchange(0, gathers=[padded])
    modulation = modulation.reshape(n_t, mod_rows * 128)[:, :mod_width].reshape(1, -1)
    pieces = [
        modulation[:, member * model_width : (member + 1) * model_width] for member in range(6)
    ]
    shift_attn, scale_attn, gate_attn, shift_feed, scale_feed, gate_feed = pieces
    residual = tokens.astype(jnp.float32)
    tangent = cotangent.astype(jnp.float32)
    normed_first, inverse_first = layer_norm(residual)
    attention_in = (normed_first * (1.0 + scale_attn) + shift_attn).astype(low)
    feed_grad = (gate_feed * tangent).astype(low)
    attention_all, feed_grad_all = exchange(1, gathers=[attention_in, feed_grad])
    query_rows = (matmul(attention_all, heads_weight[0]) + heads_bias[0]).astype(low)
    key_rows = matmul(attention_all, heads_weight[1]).astype(low)
    value_rows = (matmul(attention_all, heads_weight[2]) + heads_bias[1]).astype(low)
    mixture, logsum = attend_forward((query_rows, key_rows, value_rows))
    (branch_attn,) = exchange(2, reduces=[matmul(mixture, output_weight).astype(low)])
    branch_attn = branch_attn + output_bias
    residual_mid = residual + gate_attn * branch_attn
    normed_second, inverse_second = layer_norm(residual_mid)
    feed_in = (normed_second * (1.0 + scale_feed) + shift_feed).astype(low)
    (feed_all,) = exchange(3, gathers=[feed_in])
    hidden_pre = matmul(feed_all, first_weight) + first_bias
    activated, gelu_back = jax.vjp(partial(jax.nn.gelu, approximate=True), hidden_pre)
    activated = activated.astype(low)
    activated_grad = right_contract(feed_grad_all, second_weight)
    pre_grad = gelu_back(activated_grad)[0].astype(low)
    feed_in_grad, branch_feed = exchange(
        4,
        reduces=[
            right_contract(pre_grad, first_weight).astype(low),
            matmul(activated, second_weight).astype(low),
        ],
    )
    branch_feed = branch_feed + second_bias
    output = (residual_mid + gate_feed * branch_feed).astype(low)
    mid_grad = tangent + norm_back(feed_in_grad * (1.0 + scale_feed), normed_second, inverse_second)
    attn_grad = (gate_attn * mid_grad).astype(low)
    attn_grad_all, first_share, second_share = exchange(
        5,
        gathers=[attn_grad],
        dp_reduces=[
            left_contract(feed_all, pre_grad).astype(low),
            left_contract(feed_grad_all, activated).astype(low),
        ],
    )
    mixture_grad = right_contract(attn_grad_all, output_weight).astype(low)
    heads_grad = attend_backward((query_rows, key_rows, value_rows, mixture_grad, logsum))
    attn_in_partial = sum(right_contract(heads_grad[s], heads_weight[s]) for s in range(3))
    inner_grads = jnp.concatenate(
        [left_contract(attention_all, part).astype(low) for part in heads_grad]
        + [left_contract(attn_grad_all, mixture).astype(low)],
        axis=1,
    )
    attn_in_grad, inner_share = exchange(
        6, reduces=[attn_in_partial.astype(low)], dp_reduces=[inner_grads]
    )
    token_grad = mid_grad + norm_back(
        attn_in_grad * (1.0 + scale_attn), normed_first, inverse_first
    )
    modulation_partial = jnp.concatenate(
        [
            jnp.sum(term, axis=0)
            for term in (
                attn_in_grad,
                attn_in_grad * normed_first,
                mid_grad * branch_attn,
                feed_in_grad,
                feed_in_grad * normed_second,
                tangent * branch_feed,
            )
        ]
    )
    columns = [heads_grad[0], heads_grad[2], attn_grad_all, pre_grad, feed_grad_all]
    sums = [jnp.sum(value, axis=0, dtype=jnp.float32) for value in columns]
    vectors, modulation_all = gather_vectors(
        7, jnp.concatenate(sums + [silu_cond[0].astype(jnp.float32)]), modulation_partial
    )
    bias_total = jnp.sum(vectors, axis=0)
    offsets = [0]
    for value in sums:
        offsets.append(offsets[-1] + value.shape[0])
    bias_grads = [bias_total[offsets[i] : offsets[i + 1]] for i in range(5)]
    share = model_width // n_d
    cond_share = lax.dynamic_slice_in_dim(
        vectors[:, offsets[-1] :], lax.axis_index("dp") * share, share, 1
    )
    grad_modulate_weight = exact_left(cond_share, modulation_all)
    heads_share = inner_share[:, : 3 * local_width].reshape(share, 3, local_width)
    return (
        output,
        token_grad,
        grad_modulate_weight,
        jnp.sum(modulation_all, axis=0),
        jnp.swapaxes(heads_share, 0, 1),
        jnp.stack(bias_grads[:2]),
        inner_share[:, 3 * local_width :].T,
        bias_grads[2],
        first_share,
        bias_grads[3],
        second_share.T,
        bias_grads[4],
    )


def solution(mesh):
    in_specs = (
        P(("dp", "tensor"), None),
        P("dp", None),
        P(None, "tensor"),
        P("tensor"),
        P(None, None, "tensor"),
        P(None, "tensor"),
        P("tensor", None),
        P(),
        P(None, "tensor"),
        P("tensor"),
        P("tensor", None),
        P(),
        P(("dp", "tensor"), None),
    )
    out_specs = (
        P(("dp", "tensor"), None),
        P(("dp", "tensor"), None),
        P("dp", "tensor"),
        P("tensor"),
        P(None, "dp", "tensor"),
        P(None, "tensor"),
        P("tensor", "dp"),
        P(),
        P("dp", "tensor"),
        P("tensor"),
        P("tensor", "dp"),
        P(),
    )
    return jax.shard_map(local, mesh=mesh, in_specs=in_specs, out_specs=out_specs, check_vma=False)
```

```python
from functools import partial

import jax
import jax.numpy as jnp
from jax import lax
from jax.experimental import pallas as pl
from jax.experimental.pallas import tpu as pltpu
from jax.sharding import PartitionSpec as P

HD = 64
LEN = 512


EPSILON = 1e-06
HIGHEST_PRECISION = lax.Precision.HIGHEST


def layer_norm(values):
    centred = values - jnp.mean(values, axis=-1, keepdims=True)
    inverse = lax.rsqrt(jnp.mean(centred * centred, axis=-1, keepdims=True) + EPSILON)
    return (centred * inverse, inverse)


def norm_back(grade, normed, inverse):
    return inverse * (
        grade
        - jnp.mean(grade, axis=-1, keepdims=True)
        - normed * jnp.mean(grade * normed, axis=-1, keepdims=True)
    )


def matmul(left, right):
    return jnp.dot(left, right, preferred_element_type=jnp.float32)


def left_contract(left, right):
    return lax.dot_general(
        left, right, (((0,), (0,)), ((), ())), preferred_element_type=jnp.float32
    )


def right_contract(left, right):
    return lax.dot_general(
        left, right, (((1,), (1,)), ((), ())), preferred_element_type=jnp.float32
    )


def exact_left(left, right):
    return lax.dot_general(
        left,
        right,
        (((0,), (0,)), ((), ())),
        precision=HIGHEST_PRECISION,
        preferred_element_type=jnp.float32,
    )


def head_cols(values, head):
    return values[:, head * HD : (head + 1) * HD]


def attend_forward(blocks):
    query_block, key_block, value_block = blocks
    outputs = []
    sums = []
    for head in range(query_block.shape[1] // HD):
        scores = right_contract(head_cols(query_block, head), head_cols(key_block, head)) * HD ** (
            -0.5
        )
        peak = jnp.max(scores, axis=-1, keepdims=True)
        expo = jnp.exp(scores - peak)
        total = jnp.sum(expo, axis=-1, keepdims=True)
        probability = (expo / total).astype(jnp.bfloat16)
        outputs.append(matmul(probability, head_cols(value_block, head)))
        sums.append((peak + jnp.log(total))[:, 0])
    return (jnp.concatenate(outputs, axis=1).astype(jnp.bfloat16), jnp.stack(sums))


def attend_backward(blocks):
    query_block, key_block, value_block, grade_block, logsum = blocks
    query_parts = []
    key_parts = []
    value_parts = []
    for head in range(query_block.shape[1] // HD):
        query_head = head_cols(query_block, head)
        key_head = head_cols(key_block, head)
        grade_head = head_cols(grade_block, head)
        scores = right_contract(query_head, key_head) * HD ** (-0.5)
        probability = jnp.exp(scores - logsum[head][:, None])
        value_parts.append(left_contract(probability.astype(jnp.bfloat16), grade_head))
        prob_grad = right_contract(grade_head, head_cols(value_block, head))
        score_grad = probability * (
            prob_grad - jnp.sum(probability * prob_grad, axis=-1, keepdims=True)
        )
        score_low = score_grad.astype(jnp.bfloat16)
        query_parts.append(matmul(score_low, key_head) * HD ** (-0.5))
        key_parts.append(left_contract(score_low, query_head) * HD ** (-0.5))
    return [
        jnp.concatenate(parts, axis=1).astype(jnp.bfloat16)
        for parts in (query_parts, key_parts, value_parts)
    ]


MESH = pl.DeviceIdType.MESH
PARAMS = dict(has_side_effects=True, vmem_limit_bytes=40 * 1024 * 1024)


def greet(groups):
    barrier = pltpu.get_barrier_semaphore()
    count = 0
    for axis, peers in groups:
        for peer in peers:
            pl.semaphore_signal(barrier, inc=1, device_id={axis: peer}, device_id_type=MESH)
            count += 1
    pl.semaphore_wait(barrier, count)


def remote(src, dst, sems, slot, axis, peer):
    copy = pltpu.make_async_remote_copy(
        src_ref=src,
        dst_ref=dst,
        send_sem=sems.at[0, slot],
        recv_sem=sems.at[1, slot],
        device_id={axis: peer},
        device_id_type=MESH,
    )
    copy.start()
    return copy


PIECES = 2


def signs(rank, n_t):
    return (
        (0, 1, rank + 1 < n_t, rank > 0),
        (1, -1, rank > 0, rank + 1 < n_t),
    )


def line_copy(src, dst, sems, way, slot, piece, peer):
    return pltpu.make_async_remote_copy(
        src_ref=src,
        dst_ref=dst,
        send_sem=sems.at[0, way, slot, piece],
        recv_sem=sems.at[1, way, slot, piece],
        device_id={"tensor": peer},
        device_id_type=MESH,
    )


def inside(index, n_t):
    return jnp.logical_and(index >= 0, index < n_t)


def gather_step(rank, n_t, distance, items):
    for piece in range(PIECES):
        for way, step, ahead, behind in signs(rank, n_t):
            origin = rank - step * distance
            for src, out, sems in items:
                half = src.shape[0] // PIECES
                rows = pl.ds(pl.multiple_of(origin * src.shape[0] + piece * half, half), half)
                block = out.at[rows]
                if distance:

                    @pl.when(inside(origin, n_t))
                    def _():
                        line_copy(
                            block, block, sems, way, distance - 1, piece, rank - step
                        ).wait_recv()

                if distance < n_t - 1:

                    @pl.when(jnp.logical_and(inside(origin, n_t), ahead))
                    def _():
                        held = block if distance else src.at[pl.ds(piece * half, half)]
                        line_copy(held, block, sems, way, distance, piece, rank + step).start()


def gather_finish(rank, n_t, items):
    for distance in range(n_t - 1):
        for piece in range(PIECES):
            for way, step, ahead, behind in signs(rank, n_t):
                origin = rank - step * distance
                for src, out, sems in items:
                    half = src.shape[0] // PIECES
                    rows = pl.ds(pl.multiple_of(origin * src.shape[0] + piece * half, half), half)

                    @pl.when(jnp.logical_and(inside(origin, n_t), ahead))
                    def _():
                        held = out.at[rows] if distance else src.at[pl.ds(piece * half, half)]
                        line_copy(
                            held, out.at[rows], sems, way, distance, piece, rank + step
                        ).wait_send()


def reduce_step(rank, n_t, items, stage):
    for distance in range(n_t - 1, 0, -1):
        for piece in range(PIECES):
            for way, step, ahead, behind in signs(rank, n_t):
                target = rank + step * distance
                for src, landed, outgoing, sems in items:
                    whole = landed.shape[2]
                    half = whole // PIECES
                    rows = pl.ds(pl.multiple_of(target * whole + piece * half, half), half)
                    part = pl.ds(piece * half, half)
                    slot = distance - 1
                    ends = jnp.logical_and(inside(target, n_t), jnp.logical_not(behind))
                    inner = jnp.logical_and(inside(target, n_t), behind)

                    def make(first):
                        return line_copy(
                            src.at[rows] if first else outgoing.at[way, slot, part],
                            landed.at[way, slot, part],
                            sems,
                            way,
                            slot,
                            piece,
                            rank + step,
                        )

                    if stage == 0:

                        @pl.when(ends)
                        def _():
                            make(True).start()

                    if stage == 1 and distance < n_t - 1:

                        @pl.when(inner)
                        def _():
                            arrived = landed.at[way, distance, part]
                            line_copy(
                                arrived, arrived, sems, way, distance, piece, rank - step
                            ).wait_recv()
                            outgoing[way, slot, part, :] = (
                                src[rows, :].astype(jnp.float32)
                                + landed[way, distance, part, :].astype(jnp.float32)
                            ).astype(outgoing.dtype)
                            make(False).start()

                    if stage == 2:

                        @pl.when(ends)
                        def _():
                            make(True).wait_send()

                        if distance < n_t - 1:

                            @pl.when(inner)
                            def _():
                                make(False).wait_send()


def reduce_total(rank, n_t, items, outs):
    for (src, landed, outgoing, sems), out in zip(items, outs):
        whole = landed.shape[2]
        half = whole // PIECES
        own = pl.ds(pl.multiple_of(rank * whole, whole), whole)
        out[...] = src[own, :].astype(jnp.float32)
    for piece in range(PIECES):
        for way, step, ahead, behind in signs(rank, n_t):
            for (src, landed, outgoing, sems), out in zip(items, outs):
                half = landed.shape[2] // PIECES
                part = pl.ds(piece * half, half)

                @pl.when(behind)
                def _():
                    arrived = landed.at[way, 0, part]
                    line_copy(arrived, arrived, sems, way, 0, piece, rank - step).wait_recv()
                    out[part, :] = out[part, :] + landed[way, 0, part, :].astype(jnp.float32)


def exchange_kernel(n_t, n_d, n_gather, n_reduce, n_dp, *refs):
    refs = list(refs)

    def take(count):
        taken = refs[:count]
        del refs[:count]
        return taken

    gather_in, reduce_in, dp_in = take(n_gather), take(n_reduce), take(n_dp)
    gather_out, reduce_out, dp_out = take(n_gather), take(n_reduce), take(n_dp)
    gather_sems = take(n_gather)
    reduce_scratch = [take(3) for _ in range(n_reduce)]
    dp_scratch = [take(5) for _ in range(n_dp)]
    rank = lax.axis_index("tensor")
    t_peers = [lax.rem(rank + k, n_t) for k in range(1, n_t)]
    groups = [("tensor", t_peers)]
    n_chip = n_d // 2
    if n_dp:
        place = lax.axis_index("dp")
        chip = place // 2
        core = lax.rem(place, 2)
        chips = [lax.rem(chip + k, n_chip) for k in range(n_chip)]
        sibling = chip * 2 + 1 - core
        d_peers = [chips[k] * 2 + core for k in range(1, n_chip)]
        groups.append(("dp", [sibling] + d_peers))
    greet(groups)
    order = list(range(1, n_chip)) + [0]
    pending = []
    first_phase = []
    for src, (near, outgoing, far, near_sems, far_sems) in zip(dp_in, dp_scratch):
        first_phase.append(
            {
                k: remote(src.at[chips[k], 1 - core], near.at[k], near_sems, k, "dp", sibling)
                for k in order
            }
        )
    in_line = [
        triple for triple in zip(gather_in, gather_out, gather_sems) if len(triple[2].shape) == 4
    ]
    gathers = []
    for src, dst, sems in zip(gather_in, gather_out, gather_sems):
        if len(sems.shape) == 2:
            rows = src.shape[0]
            own = pl.ds(pl.multiple_of(rank * rows, rows), rows)
            for k, peer in enumerate(t_peers):
                gathers.append(remote(src, dst.at[own], sems, k, "tensor", peer))
    reduces = [(src, *scratch) for src, scratch in zip(reduce_in, reduce_scratch)]
    gather_step(rank, n_t, 0, in_line)
    reduce_step(rank, n_t, reduces, 0)
    second_phase = []
    for src, out, copies, (near, outgoing, far, near_sems, far_sems) in zip(
        dp_in, dp_out, first_phase, dp_scratch
    ):
        later = []
        for k in order:
            copies[k].wait_recv()
            value = src[chips[k], core].astype(jnp.float32) + near[k].astype(jnp.float32)
            if k == 0:
                out[...] = value
            else:
                outgoing[k - 1] = value.astype(outgoing.dtype)
                later.append(
                    remote(
                        outgoing.at[k - 1], far.at[k - 1], far_sems, k - 1, "dp", d_peers[k - 1]
                    )
                )
        second_phase.append(later)
    for src, dst in zip(gather_in, gather_out):
        rows = src.shape[0]
        dst[pl.ds(pl.multiple_of(rank * rows, rows), rows), :] = src[...]
    reduce_step(rank, n_t, reduces, 1)
    for distance in range(1, n_t):
        gather_step(rank, n_t, distance, in_line)
    reduce_total(rank, n_t, reduces, reduce_out)
    for copy in gathers:
        copy.wait_recv()
    for out, later, scratch in zip(dp_out, second_phase, dp_scratch):
        total = out[...]
        for k, copy in enumerate(later):
            copy.wait_recv()
            total = total + scratch[2][k].astype(jnp.float32)
        out[...] = total
    for copy in gathers:
        copy.wait_send()
    gather_finish(rank, n_t, in_line)
    reduce_step(rank, n_t, reduces, 2)
    for copies in second_phase:
        for copy in copies:
            copy.wait_send()
    for copies in first_phase:
        for k in order:
            copies[k].wait_send()


def exchange(ident, gathers=(), reduces=(), dp_reduces=()):
    n_t, n_d = lax.axis_size("tensor"), lax.axis_size("dp")
    n_chip = n_d // 2
    outs = []
    scratch = []
    by_kernel = n_d <= 8 and n_d % 2 == 0
    inputs = list(gathers) + list(reduces)
    for value in gathers:
        outs.append(jax.ShapeDtypeStruct((n_t * value.shape[0], value.shape[1]), value.dtype))
        lined = value.shape[0] % (16 * PIECES) == 0
        shape = (2, 2, n_t - 1, PIECES) if lined else (2, n_t - 1)
        scratch.append(pltpu.SemaphoreType.DMA(shape))
    for value in reduces:
        rows, columns = value.shape[0] // n_t, value.shape[1]
        outs.append(jax.ShapeDtypeStruct((rows, columns), jnp.float32))
        scratch.append(pltpu.VMEM((2, n_t - 1, rows, columns), value.dtype))
        scratch.append(pltpu.VMEM((2, n_t - 1, rows, columns), value.dtype))
        scratch.append(pltpu.SemaphoreType.DMA((2, 2, n_t - 1, PIECES)))
    n_dp = 0
    if by_kernel:
        for value in dp_reduces:
            rows, columns = value.shape[0] // n_d, value.shape[1]
            n_dp += 1
            inputs.append(value.reshape(n_chip, 2, rows, columns))
            outs.append(jax.ShapeDtypeStruct((rows, columns), jnp.float32))
            scratch += [
                pltpu.VMEM((n_chip, rows, columns), value.dtype),
                pltpu.VMEM((n_chip - 1, rows, columns), value.dtype),
                pltpu.VMEM((n_chip - 1, rows, columns), value.dtype),
                pltpu.SemaphoreType.DMA((2, n_chip)),
                pltpu.SemaphoreType.DMA((2, n_chip - 1)),
            ]
    results = pl.pallas_call(
        partial(exchange_kernel, n_t, n_d, len(gathers), len(reduces), n_dp),
        out_shape=outs,
        in_specs=[pl.BlockSpec(memory_space=pltpu.VMEM)] * len(inputs),
        out_specs=[pl.BlockSpec(memory_space=pltpu.VMEM)] * len(outs),
        scratch_shapes=scratch,
        compiler_params=pltpu.CompilerParams(collective_id=ident, **PARAMS),
        name="exchange_%d" % ident,
    )(*inputs)
    if not by_kernel:
        results = list(results) + [
            lax.psum_scatter(value.astype(jnp.float32), "dp", scatter_dimension=0, tiled=True)
            for value in dp_reduces
        ]
    return results


def vector_kernel(n_t, n_d, first, shares, first_all, share_all, landed, total, *sems):
    first_sems, part_sems, total_sems = sems
    rank, place = lax.axis_index("tensor"), lax.axis_index("dp")
    t_peers = [lax.rem(rank + k, n_t) for k in range(1, n_t)]
    d_peers = [lax.rem(place + k, n_d) for k in range(1, n_d)]
    greet([("tensor", t_peers), ("dp", d_peers)])
    parts = [
        remote(shares.at[peer], landed.at[k], part_sems, k, "tensor", peer)
        for k, peer in enumerate(t_peers)
    ]
    copies = [
        remote(first, first_all.at[place], first_sems, k, "dp", peer)
        for k, peer in enumerate(d_peers)
    ]
    value = shares[rank]
    for k, copy in enumerate(parts):
        copy.wait_recv()
        value = value + landed[k]
    total[...] = value
    copies += [
        remote(total, share_all.at[place], total_sems, k, "dp", peer)
        for k, peer in enumerate(d_peers)
    ]
    share_all[place] = value
    first_all[place] = first[...]
    for copy in copies:
        copy.wait_recv()
    for copy in copies + parts:
        copy.wait_send()


def gather_vectors(ident, first, shares):
    n_t, n_d = lax.axis_size("tensor"), lax.axis_size("dp")
    if n_d > 8:
        total = lax.psum_scatter(shares, "tensor", scatter_dimension=0, tiled=True)
        return (lax.all_gather(first, "dp"), lax.all_gather(total, "dp"))
    length, width = first.shape[0], shares.shape[0] // n_t
    length_rows, width_rows = -(-length // 1024) * 8, -(-width // 1024) * 8
    first = jnp.pad(first, (0, length_rows * 128 - length)).reshape(length_rows, 128)
    shares = jnp.pad(shares.reshape(n_t, width), ((0, 0), (0, width_rows * 128 - width)))
    shares = shares.reshape(n_t, width_rows, 128)
    first_all, share_all = pl.pallas_call(
        partial(vector_kernel, n_t, n_d),
        out_shape=[
            jax.ShapeDtypeStruct((n_d, length_rows, 128), jnp.float32),
            jax.ShapeDtypeStruct((n_d, width_rows, 128), jnp.float32),
        ],
        in_specs=[pl.BlockSpec(memory_space=pltpu.VMEM)] * 2,
        out_specs=[pl.BlockSpec(memory_space=pltpu.VMEM)] * 2,
        scratch_shapes=[
            pltpu.VMEM((n_t - 1, width_rows, 128), jnp.float32),
            pltpu.VMEM((width_rows, 128), jnp.float32),
            pltpu.SemaphoreType.DMA((2, n_d - 1)),
            pltpu.SemaphoreType.DMA((2, n_t - 1)),
            pltpu.SemaphoreType.DMA((2, n_d - 1)),
        ],
        compiler_params=pltpu.CompilerParams(collective_id=ident, **PARAMS),
        name="gather_vectors",
    )(first, shares)
    return (
        first_all.reshape(n_d, -1)[:, :length],
        share_all.reshape(n_d, -1)[:, :width],
    )


def local(
    tokens,
    condition,
    modulate_weight,
    modulate_bias,
    heads_weight,
    heads_bias,
    output_weight,
    output_bias,
    first_weight,
    first_bias,
    second_weight,
    second_bias,
    cotangent,
):
    row_count, model_width = tokens.shape
    n_t, n_d = lax.axis_size("tensor"), lax.axis_size("dp")
    local_width = heads_weight.shape[2]
    assert condition.shape[0] == 1 and n_t * row_count == LEN
    low = jnp.bfloat16
    silu_cond = jax.nn.silu(condition.astype(jnp.float32)).astype(low)
    modulate_local = matmul(silu_cond, modulate_weight) + modulate_bias
    mod_width = modulate_local.shape[1]
    mod_rows = -(-mod_width // 1024) * 8
    padded = jnp.pad(modulate_local[0], (0, mod_rows * 128 - mod_width)).reshape(mod_rows, 128)
    (modulation,) = exchange(0, gathers=[padded])
    modulation = modulation.reshape(n_t, mod_rows * 128)[:, :mod_width].reshape(1, -1)
    pieces = [
        modulation[:, member * model_width : (member + 1) * model_width] for member in range(6)
    ]
    shift_attn, scale_attn, gate_attn, shift_feed, scale_feed, gate_feed = pieces
    residual = tokens.astype(jnp.float32)
    tangent = cotangent.astype(jnp.float32)
    normed_first, inverse_first = layer_norm(residual)
    attention_in = (normed_first * (1.0 + scale_attn) + shift_attn).astype(low)
    feed_grad = (gate_feed * tangent).astype(low)
    attention_all, feed_grad_all = exchange(1, gathers=[attention_in, feed_grad])
    query_rows = (matmul(attention_all, heads_weight[0]) + heads_bias[0]).astype(low)
    key_rows = matmul(attention_all, heads_weight[1]).astype(low)
    value_rows = (matmul(attention_all, heads_weight[2]) + heads_bias[1]).astype(low)
    mixture, logsum = attend_forward((query_rows, key_rows, value_rows))
    (branch_attn,) = exchange(2, reduces=[matmul(mixture, output_weight).astype(low)])
    branch_attn = branch_attn + output_bias
    residual_mid = residual + gate_attn * branch_attn
    normed_second, inverse_second = layer_norm(residual_mid)
    feed_in = (normed_second * (1.0 + scale_feed) + shift_feed).astype(low)
    (feed_all,) = exchange(3, gathers=[feed_in])
    hidden_pre = matmul(feed_all, first_weight) + first_bias
    activated, gelu_back = jax.vjp(partial(jax.nn.gelu, approximate=True), hidden_pre)
    activated = activated.astype(low)
    activated_grad = right_contract(feed_grad_all, second_weight)
    pre_grad = gelu_back(activated_grad)[0].astype(low)
    feed_in_grad, branch_feed = exchange(
        4,
        reduces=[
            right_contract(pre_grad, first_weight).astype(low),
            matmul(activated, second_weight).astype(low),
        ],
    )
    branch_feed = branch_feed + second_bias
    output = (residual_mid + gate_feed * branch_feed).astype(low)
    mid_grad = tangent + norm_back(feed_in_grad * (1.0 + scale_feed), normed_second, inverse_second)
    attn_grad = (gate_attn * mid_grad).astype(low)
    attn_grad_all, first_share, second_share = exchange(
        5,
        gathers=[attn_grad],
        dp_reduces=[
            left_contract(feed_all, pre_grad).astype(low),
            left_contract(feed_grad_all, activated).astype(low),
        ],
    )
    mixture_grad = right_contract(attn_grad_all, output_weight).astype(low)
    heads_grad = attend_backward((query_rows, key_rows, value_rows, mixture_grad, logsum))
    attn_in_partial = sum(right_contract(heads_grad[s], heads_weight[s]) for s in range(3))
    inner_grads = jnp.concatenate(
        [left_contract(attention_all, part).astype(low) for part in heads_grad]
        + [left_contract(attn_grad_all, mixture).astype(low)],
        axis=1,
    )
    attn_in_grad, inner_share = exchange(
        6, reduces=[attn_in_partial.astype(low)], dp_reduces=[inner_grads]
    )
    token_grad = mid_grad + norm_back(
        attn_in_grad * (1.0 + scale_attn), normed_first, inverse_first
    )
    modulation_partial = jnp.concatenate(
        [
            jnp.sum(term, axis=0)
            for term in (
                attn_in_grad,
                attn_in_grad * normed_first,
                mid_grad * branch_attn,
                feed_in_grad,
                feed_in_grad * normed_second,
                tangent * branch_feed,
            )
        ]
    )
    columns = [heads_grad[0], heads_grad[2], attn_grad_all, pre_grad, feed_grad_all]
    sums = [jnp.sum(value, axis=0, dtype=jnp.float32) for value in columns]
    vectors, modulation_all = gather_vectors(
        7, jnp.concatenate(sums + [silu_cond[0].astype(jnp.float32)]), modulation_partial
    )
    bias_total = jnp.sum(vectors, axis=0)
    offsets = [0]
    for value in sums:
        offsets.append(offsets[-1] + value.shape[0])
    bias_grads = [bias_total[offsets[i] : offsets[i + 1]] for i in range(5)]
    share = model_width // n_d
    cond_share = lax.dynamic_slice_in_dim(
        vectors[:, offsets[-1] :], lax.axis_index("dp") * share, share, 1
    )
    grad_modulate_weight = exact_left(cond_share, modulation_all)
    heads_share = inner_share[:, : 3 * local_width].reshape(share, 3, local_width)
    return (
        output,
        token_grad,
        grad_modulate_weight,
        jnp.sum(modulation_all, axis=0),
        jnp.swapaxes(heads_share, 0, 1),
        jnp.stack(bias_grads[:2]),
        inner_share[:, 3 * local_width :].T,
        bias_grads[2],
        first_share,
        bias_grads[3],
        second_share.T,
        bias_grads[4],
    )


def solution(mesh):
    in_specs = (
        P(("dp", "tensor"), None),
        P("dp", None),
        P(None, "tensor"),
        P("tensor"),
        P(None, None, "tensor"),
        P(None, "tensor"),
        P("tensor", None),
        P(),
        P(None, "tensor"),
        P("tensor"),
        P("tensor", None),
        P(),
        P(("dp", "tensor"), None),
    )
    out_specs = (
        P(("dp", "tensor"), None),
        P(("dp", "tensor"), None),
        P("dp", "tensor"),
        P("tensor"),
        P(None, "dp", "tensor"),
        P(None, "tensor"),
        P("tensor", "dp"),
        P(),
        P("dp", "tensor"),
        P("tensor"),
        P("tensor", "dp"),
        P(),
    )
    return jax.shard_map(local, mesh=mesh, in_specs=in_specs, out_specs=out_specs, check_vma=False)
```

```python
from functools import partial

import jax
import jax.numpy as jnp
from jax import lax
from jax.experimental import pallas as pl
from jax.experimental.pallas import tpu as pltpu
from jax.sharding import PartitionSpec as P

HD = 64
LEN = 512


EPSILON = 1e-06
HIGHEST_PRECISION = lax.Precision.HIGHEST


def layer_norm(values):
    centred = values - jnp.mean(values, axis=-1, keepdims=True)
    inverse = lax.rsqrt(jnp.mean(centred * centred, axis=-1, keepdims=True) + EPSILON)
    return (centred * inverse, inverse)


def norm_back(grade, normed, inverse):
    return inverse * (
        grade
        - jnp.mean(grade, axis=-1, keepdims=True)
        - normed * jnp.mean(grade * normed, axis=-1, keepdims=True)
    )


def matmul(left, right):
    return jnp.dot(left, right, preferred_element_type=jnp.float32)


def left_contract(left, right):
    return lax.dot_general(
        left, right, (((0,), (0,)), ((), ())), preferred_element_type=jnp.float32
    )


def right_contract(left, right):
    return lax.dot_general(
        left, right, (((1,), (1,)), ((), ())), preferred_element_type=jnp.float32
    )


def exact_left(left, right):
    return lax.dot_general(
        left,
        right,
        (((0,), (0,)), ((), ())),
        precision=HIGHEST_PRECISION,
        preferred_element_type=jnp.float32,
    )


def head_cols(values, head):
    return values[:, head * HD : (head + 1) * HD]


def attend_forward(blocks):
    query_block, key_block, value_block = blocks
    outputs = []
    sums = []
    for head in range(query_block.shape[1] // HD):
        scores = right_contract(head_cols(query_block, head), head_cols(key_block, head)) * HD ** (
            -0.5
        )
        peak = jnp.max(scores, axis=-1, keepdims=True)
        expo = jnp.exp(scores - peak)
        total = jnp.sum(expo, axis=-1, keepdims=True)
        probability = (expo / total).astype(jnp.bfloat16)
        outputs.append(matmul(probability, head_cols(value_block, head)))
        sums.append((peak + jnp.log(total))[:, 0])
    return (jnp.concatenate(outputs, axis=1).astype(jnp.bfloat16), jnp.stack(sums))


def attend_backward(blocks):
    query_block, key_block, value_block, grade_block, logsum = blocks
    query_parts = []
    key_parts = []
    value_parts = []
    for head in range(query_block.shape[1] // HD):
        query_head = head_cols(query_block, head)
        key_head = head_cols(key_block, head)
        grade_head = head_cols(grade_block, head)
        scores = right_contract(query_head, key_head) * HD ** (-0.5)
        probability = jnp.exp(scores - logsum[head][:, None])
        value_parts.append(left_contract(probability.astype(jnp.bfloat16), grade_head))
        prob_grad = right_contract(grade_head, head_cols(value_block, head))
        score_grad = probability * (
            prob_grad - jnp.sum(probability * prob_grad, axis=-1, keepdims=True)
        )
        score_low = score_grad.astype(jnp.bfloat16)
        query_parts.append(matmul(score_low, key_head) * HD ** (-0.5))
        key_parts.append(left_contract(score_low, query_head) * HD ** (-0.5))
    return [
        jnp.concatenate(parts, axis=1).astype(jnp.bfloat16)
        for parts in (query_parts, key_parts, value_parts)
    ]


MESH = pl.DeviceIdType.MESH
PARAMS = dict(has_side_effects=True, vmem_limit_bytes=40 * 1024 * 1024)


def greet(groups):
    barrier = pltpu.get_barrier_semaphore()
    count = 0
    for axis, peers in groups:
        for peer in peers:
            pl.semaphore_signal(barrier, inc=1, device_id={axis: peer}, device_id_type=MESH)
            count += 1
    pl.semaphore_wait(barrier, count)


def remote(src, dst, sems, slot, axis, peer):
    copy = pltpu.make_async_remote_copy(
        src_ref=src,
        dst_ref=dst,
        send_sem=sems.at[0, slot],
        recv_sem=sems.at[1, slot],
        device_id={axis: peer},
        device_id_type=MESH,
    )
    copy.start()
    return copy


PIECES = 2


def signs(rank, n_t):
    return (
        (0, 1, rank + 1 < n_t, rank > 0),
        (1, -1, rank > 0, rank + 1 < n_t),
    )


def line_copy(src, dst, sems, way, slot, piece, peer):
    return pltpu.make_async_remote_copy(
        src_ref=src,
        dst_ref=dst,
        send_sem=sems.at[0, way, slot, piece],
        recv_sem=sems.at[1, way, slot, piece],
        device_id={"tensor": peer},
        device_id_type=MESH,
    )


def inside(index, n_t):
    return jnp.logical_and(index >= 0, index < n_t)


def gather_step(rank, n_t, distance, items):
    for piece in range(PIECES):
        for way, step, ahead, behind in signs(rank, n_t):
            origin = rank - step * distance
            for src, out, sems in items:
                half = src.shape[0] // PIECES
                rows = pl.ds(pl.multiple_of(origin * src.shape[0] + piece * half, half), half)
                block = out.at[rows]
                if distance:

                    @pl.when(inside(origin, n_t))
                    def _():
                        line_copy(
                            block, block, sems, way, distance - 1, piece, rank - step
                        ).wait_recv()

                if distance < n_t - 1:

                    @pl.when(jnp.logical_and(inside(origin, n_t), ahead))
                    def _():
                        held = block if distance else src.at[pl.ds(piece * half, half)]
                        line_copy(held, block, sems, way, distance, piece, rank + step).start()


def gather_finish(rank, n_t, items):
    for distance in range(n_t - 1):
        for piece in range(PIECES):
            for way, step, ahead, behind in signs(rank, n_t):
                origin = rank - step * distance
                for src, out, sems in items:
                    half = src.shape[0] // PIECES
                    rows = pl.ds(pl.multiple_of(origin * src.shape[0] + piece * half, half), half)

                    @pl.when(jnp.logical_and(inside(origin, n_t), ahead))
                    def _():
                        held = out.at[rows] if distance else src.at[pl.ds(piece * half, half)]
                        line_copy(
                            held, out.at[rows], sems, way, distance, piece, rank + step
                        ).wait_send()


def reduce_step(rank, n_t, items, stage):
    for distance in range(n_t - 1, 0, -1):
        for piece in range(PIECES):
            for way, step, ahead, behind in signs(rank, n_t):
                target = rank + step * distance
                for src, landed, outgoing, sems in items:
                    whole = landed.shape[2]
                    half = whole // PIECES
                    rows = pl.ds(pl.multiple_of(target * whole + piece * half, half), half)
                    part = pl.ds(piece * half, half)
                    slot = distance - 1
                    ends = jnp.logical_and(inside(target, n_t), jnp.logical_not(behind))
                    inner = jnp.logical_and(inside(target, n_t), behind)

                    def make(first):
                        return line_copy(
                            src.at[rows] if first else outgoing.at[way, slot, part],
                            landed.at[way, slot, part],
                            sems,
                            way,
                            slot,
                            piece,
                            rank + step,
                        )

                    if stage == 0:

                        @pl.when(ends)
                        def _():
                            make(True).start()

                    if stage == 1 and distance < n_t - 1:

                        @pl.when(inner)
                        def _():
                            arrived = landed.at[way, distance, part]
                            line_copy(
                                arrived, arrived, sems, way, distance, piece, rank - step
                            ).wait_recv()
                            outgoing[way, slot, part, :] = (
                                src[rows, :].astype(jnp.float32)
                                + landed[way, distance, part, :].astype(jnp.float32)
                            ).astype(outgoing.dtype)
                            make(False).start()

                    if stage == 2:

                        @pl.when(ends)
                        def _():
                            make(True).wait_send()

                        if distance < n_t - 1:

                            @pl.when(inner)
                            def _():
                                make(False).wait_send()


def reduce_total(rank, n_t, items, outs):
    for (src, landed, outgoing, sems), out in zip(items, outs):
        whole = landed.shape[2]
        half = whole // PIECES
        own = pl.ds(pl.multiple_of(rank * whole, whole), whole)
        out[...] = src[own, :].astype(jnp.float32)
    for piece in range(PIECES):
        for way, step, ahead, behind in signs(rank, n_t):
            for (src, landed, outgoing, sems), out in zip(items, outs):
                half = landed.shape[2] // PIECES
                part = pl.ds(piece * half, half)

                @pl.when(behind)
                def _():
                    arrived = landed.at[way, 0, part]
                    line_copy(arrived, arrived, sems, way, 0, piece, rank - step).wait_recv()
                    out[part, :] = out[part, :] + landed[way, 0, part, :].astype(jnp.float32)


def exchange_kernel(n_t, n_d, n_gather, n_reduce, n_dp, *refs):
    refs = list(refs)

    def take(count):
        taken = refs[:count]
        del refs[:count]
        return taken

    gather_in, reduce_in, dp_in = take(n_gather), take(n_reduce), take(n_dp)
    gather_out, reduce_out, dp_out = take(n_gather), take(n_reduce), take(n_dp)
    gather_sems = take(n_gather)
    reduce_scratch = [take(3) for _ in range(n_reduce)]
    dp_scratch = [take(5) for _ in range(n_dp)]
    rank = lax.axis_index("tensor")
    t_peers = [lax.rem(rank + k, n_t) for k in range(1, n_t)]
    groups = [("tensor", t_peers)]
    n_chip = n_d // 2
    if n_dp:
        place = lax.axis_index("dp")
        chip = place // 2
        core = lax.rem(place, 2)
        chips = [lax.rem(chip + k, n_chip) for k in range(n_chip)]
        sibling = chip * 2 + 1 - core
        d_peers = [chips[k] * 2 + core for k in range(1, n_chip)]
        groups.append(("dp", [sibling] + d_peers))
    greet(groups)
    order = list(range(1, n_chip)) + [0]
    pending = []
    first_phase = []
    for src, (near, outgoing, far, near_sems, far_sems) in zip(dp_in, dp_scratch):
        first_phase.append(
            {
                k: remote(src.at[chips[k], 1 - core], near.at[k], near_sems, k, "dp", sibling)
                for k in order
            }
        )
    in_line = [
        triple for triple in zip(gather_in, gather_out, gather_sems) if len(triple[2].shape) == 4
    ]
    gathers = []
    for src, dst, sems in zip(gather_in, gather_out, gather_sems):
        if len(sems.shape) == 2:
            rows = src.shape[0]
            own = pl.ds(pl.multiple_of(rank * rows, rows), rows)
            for k, peer in enumerate(t_peers):
                gathers.append(remote(src, dst.at[own], sems, k, "tensor", peer))
    reduces = [(src, *scratch) for src, scratch in zip(reduce_in, reduce_scratch)]
    gather_step(rank, n_t, 0, in_line)
    reduce_step(rank, n_t, reduces, 0)
    second_phase = []
    for src, out, copies, (near, outgoing, far, near_sems, far_sems) in zip(
        dp_in, dp_out, first_phase, dp_scratch
    ):
        later = []
        for k in order:
            copies[k].wait_recv()
            value = src[chips[k], core].astype(jnp.float32) + near[k].astype(jnp.float32)
            if k == 0:
                out[...] = value
            else:
                outgoing[k - 1] = value.astype(outgoing.dtype)
                later.append(
                    remote(
                        outgoing.at[k - 1], far.at[k - 1], far_sems, k - 1, "dp", d_peers[k - 1]
                    )
                )
        second_phase.append(later)
    for src, dst in zip(gather_in, gather_out):
        rows = src.shape[0]
        dst[pl.ds(pl.multiple_of(rank * rows, rows), rows), :] = src[...]
    reduce_step(rank, n_t, reduces, 1)
    for distance in range(1, n_t):
        gather_step(rank, n_t, distance, in_line)
    reduce_total(rank, n_t, reduces, reduce_out)
    for copy in gathers:
        copy.wait_recv()
    for out, later, scratch in zip(dp_out, second_phase, dp_scratch):
        total = out[...]
        for k, copy in enumerate(later):
            copy.wait_recv()
            total = total + scratch[2][k].astype(jnp.float32)
        out[...] = total
    for copy in gathers:
        copy.wait_send()
    gather_finish(rank, n_t, in_line)
    reduce_step(rank, n_t, reduces, 2)
    for copies in second_phase:
        for copy in copies:
            copy.wait_send()
    for copies in first_phase:
        for k in order:
            copies[k].wait_send()


def exchange(ident, gathers=(), reduces=(), dp_reduces=()):
    n_t, n_d = lax.axis_size("tensor"), lax.axis_size("dp")
    n_chip = n_d // 2
    outs = []
    scratch = []
    by_kernel = n_d <= 8 and n_d % 2 == 0
    inputs = list(gathers) + list(reduces)
    for value in gathers:
        outs.append(jax.ShapeDtypeStruct((n_t * value.shape[0], value.shape[1]), value.dtype))
        lined = value.shape[0] % (16 * PIECES) == 0
        shape = (2, 2, n_t - 1, PIECES) if lined else (2, n_t - 1)
        scratch.append(pltpu.SemaphoreType.DMA(shape))
    for value in reduces:
        rows, columns = value.shape[0] // n_t, value.shape[1]
        outs.append(jax.ShapeDtypeStruct((rows, columns), jnp.float32))
        scratch.append(pltpu.VMEM((2, n_t - 1, rows, columns), value.dtype))
        scratch.append(pltpu.VMEM((2, n_t - 1, rows, columns), value.dtype))
        scratch.append(pltpu.SemaphoreType.DMA((2, 2, n_t - 1, PIECES)))
    n_dp = 0
    if by_kernel:
        for value in dp_reduces:
            rows, columns = value.shape[0] // n_d, value.shape[1]
            n_dp += 1
            inputs.append(value.reshape(n_chip, 2, rows, columns))
            outs.append(jax.ShapeDtypeStruct((rows, columns), jnp.float32))
            scratch += [
                pltpu.VMEM((n_chip, rows, columns), value.dtype),
                pltpu.VMEM((n_chip - 1, rows, columns), value.dtype),
                pltpu.VMEM((n_chip - 1, rows, columns), value.dtype),
                pltpu.SemaphoreType.DMA((2, n_chip)),
                pltpu.SemaphoreType.DMA((2, n_chip - 1)),
            ]
    results = pl.pallas_call(
        partial(exchange_kernel, n_t, n_d, len(gathers), len(reduces), n_dp),
        out_shape=outs,
        in_specs=[pl.BlockSpec(memory_space=pltpu.VMEM)] * len(inputs),
        out_specs=[pl.BlockSpec(memory_space=pltpu.VMEM)] * len(outs),
        scratch_shapes=scratch,
        compiler_params=pltpu.CompilerParams(collective_id=ident, **PARAMS),
        name="exchange_%d" % ident,
    )(*inputs)
    if not by_kernel:
        results = list(results) + [
            lax.psum_scatter(value.astype(jnp.float32), "dp", scatter_dimension=0, tiled=True)
            for value in dp_reduces
        ]
    return results


def row_terms(grade_a, normed_a, mid, branch_a, grade_f, normed_f, tangent, branch_f):
    return (
        grade_a,
        grade_a * normed_a,
        mid * branch_a,
        grade_f,
        grade_f * normed_f,
        tangent * branch_f,
    )


def vector_kernel(n_t, n_d, lanes, first, *refs):
    rows, (first_all, share_all, shares, landed, total, *sems) = refs[:8], refs[8:]
    first_sems, part_sems, total_sems = sems
    rank, place = lax.axis_index("tensor"), lax.axis_index("dp")
    t_peers = [lax.rem(rank + k, n_t) for k in range(1, n_t)]
    d_peers = [lax.rem(place + k, n_d) for k in range(1, n_d)]
    greet([("tensor", t_peers), ("dp", d_peers)])
    copies = [
        remote(first, first_all.at[place], first_sems, k, "dp", peer)
        for k, peer in enumerate(d_peers)
    ]
    shares[...] = jnp.zeros_like(shares)
    for member, term in enumerate(row_terms(*[ref[...].astype(jnp.float32) for ref in rows])):
        line = jnp.sum(term, axis=0, keepdims=True)
        per_member = line.shape[1] // 128
        for i in range(per_member):
            owner, row = divmod(member * per_member + i, lanes)
            shares[owner, row : row + 1, :] = line[:, i * 128 : (i + 1) * 128]
    parts = [
        remote(shares.at[peer], landed.at[k], part_sems, k, "tensor", peer)
        for k, peer in enumerate(t_peers)
    ]
    value = shares[rank]
    for k, copy in enumerate(parts):
        copy.wait_recv()
        value = value + landed[k]
    total[...] = value
    copies += [
        remote(total, share_all.at[place], total_sems, k, "dp", peer)
        for k, peer in enumerate(d_peers)
    ]
    share_all[place] = value
    first_all[place] = first[...]
    for copy in copies:
        copy.wait_recv()
    for copy in copies + parts:
        copy.wait_send()


def gather_vectors(ident, first, rows):
    n_t, n_d = lax.axis_size("tensor"), lax.axis_size("dp")
    if n_d > 8 or rows[0].shape[1] % 128 or 6 * rows[0].shape[1] % (n_t * 128):
        terms = row_terms(*[value.astype(jnp.float32) for value in rows])
        shares = jnp.concatenate([jnp.sum(term, axis=0) for term in terms])
        total = lax.psum_scatter(shares, "tensor", scatter_dimension=0, tiled=True)
        return (lax.all_gather(first, "dp"), lax.all_gather(total, "dp"))
    length, width = first.shape[0], 6 * rows[0].shape[1] // n_t
    length_rows, width_rows = -(-length // 1024) * 8, -(-width // 1024) * 8
    first = jnp.pad(first, (0, length_rows * 128 - length)).reshape(length_rows, 128)
    first_all, share_all = pl.pallas_call(
        partial(vector_kernel, n_t, n_d, width // 128),
        out_shape=[
            jax.ShapeDtypeStruct((n_d, length_rows, 128), jnp.float32),
            jax.ShapeDtypeStruct((n_d, width_rows, 128), jnp.float32),
        ],
        in_specs=[pl.BlockSpec(memory_space=pltpu.VMEM)] * 9,
        out_specs=[pl.BlockSpec(memory_space=pltpu.VMEM)] * 2,
        scratch_shapes=[
            pltpu.VMEM((n_t, width_rows, 128), jnp.float32),
            pltpu.VMEM((n_t - 1, width_rows, 128), jnp.float32),
            pltpu.VMEM((width_rows, 128), jnp.float32),
            pltpu.SemaphoreType.DMA((2, n_d - 1)),
            pltpu.SemaphoreType.DMA((2, n_t - 1)),
            pltpu.SemaphoreType.DMA((2, n_d - 1)),
        ],
        compiler_params=pltpu.CompilerParams(collective_id=ident, **PARAMS),
        name="gather_vectors",
    )(first, *rows)
    return (
        first_all.reshape(n_d, -1)[:, :length],
        share_all.reshape(n_d, -1)[:, :width],
    )


def local(
    tokens,
    condition,
    modulate_weight,
    modulate_bias,
    heads_weight,
    heads_bias,
    output_weight,
    output_bias,
    first_weight,
    first_bias,
    second_weight,
    second_bias,
    cotangent,
):
    row_count, model_width = tokens.shape
    n_t, n_d = lax.axis_size("tensor"), lax.axis_size("dp")
    local_width = heads_weight.shape[2]
    assert condition.shape[0] == 1 and n_t * row_count == LEN
    low = jnp.bfloat16
    silu_cond = jax.nn.silu(condition.astype(jnp.float32)).astype(low)
    modulate_local = matmul(silu_cond, modulate_weight) + modulate_bias
    mod_width = modulate_local.shape[1]
    mod_rows = -(-mod_width // 1024) * 8
    padded = jnp.pad(modulate_local[0], (0, mod_rows * 128 - mod_width)).reshape(mod_rows, 128)
    (modulation,) = exchange(0, gathers=[padded])
    modulation = modulation.reshape(n_t, mod_rows * 128)[:, :mod_width].reshape(1, -1)
    pieces = [
        modulation[:, member * model_width : (member + 1) * model_width] for member in range(6)
    ]
    shift_attn, scale_attn, gate_attn, shift_feed, scale_feed, gate_feed = pieces
    residual = tokens.astype(jnp.float32)
    tangent = cotangent.astype(jnp.float32)
    normed_first, inverse_first = layer_norm(residual)
    attention_in = (normed_first * (1.0 + scale_attn) + shift_attn).astype(low)
    feed_grad = (gate_feed * tangent).astype(low)
    attention_all, feed_grad_all = exchange(1, gathers=[attention_in, feed_grad])
    query_rows = (matmul(attention_all, heads_weight[0]) + heads_bias[0]).astype(low)
    key_rows = matmul(attention_all, heads_weight[1]).astype(low)
    value_rows = (matmul(attention_all, heads_weight[2]) + heads_bias[1]).astype(low)
    mixture, logsum = attend_forward((query_rows, key_rows, value_rows))
    (branch_attn,) = exchange(2, reduces=[matmul(mixture, output_weight).astype(low)])
    branch_attn = branch_attn + output_bias
    residual_mid = residual + gate_attn * branch_attn
    normed_second, inverse_second = layer_norm(residual_mid)
    feed_in = (normed_second * (1.0 + scale_feed) + shift_feed).astype(low)
    (feed_all,) = exchange(3, gathers=[feed_in])
    hidden_pre = matmul(feed_all, first_weight) + first_bias
    activated, gelu_back = jax.vjp(partial(jax.nn.gelu, approximate=True), hidden_pre)
    activated = activated.astype(low)
    activated_grad = right_contract(feed_grad_all, second_weight)
    pre_grad = gelu_back(activated_grad)[0].astype(low)
    feed_in_grad, branch_feed = exchange(
        4,
        reduces=[
            right_contract(pre_grad, first_weight).astype(low),
            matmul(activated, second_weight).astype(low),
        ],
    )
    branch_feed = branch_feed + second_bias
    output = (residual_mid + gate_feed * branch_feed).astype(low)
    mid_grad = tangent + norm_back(feed_in_grad * (1.0 + scale_feed), normed_second, inverse_second)
    attn_grad = (gate_attn * mid_grad).astype(low)
    attn_grad_all, first_share, second_share = exchange(
        5,
        gathers=[attn_grad],
        dp_reduces=[
            left_contract(feed_all, pre_grad).astype(low),
            left_contract(feed_grad_all, activated).astype(low),
        ],
    )
    mixture_grad = right_contract(attn_grad_all, output_weight).astype(low)
    heads_grad = attend_backward((query_rows, key_rows, value_rows, mixture_grad, logsum))
    attn_in_partial = sum(right_contract(heads_grad[s], heads_weight[s]) for s in range(3))
    inner_grads = jnp.concatenate(
        [left_contract(attention_all, part).astype(low) for part in heads_grad]
        + [left_contract(attn_grad_all, mixture).astype(low)],
        axis=1,
    )
    attn_in_grad, inner_share = exchange(
        6, reduces=[attn_in_partial.astype(low)], dp_reduces=[inner_grads]
    )
    token_grad = mid_grad + norm_back(
        attn_in_grad * (1.0 + scale_attn), normed_first, inverse_first
    )
    rows = (
        attn_in_grad,
        normed_first,
        mid_grad,
        branch_attn,
        feed_in_grad,
        normed_second,
        cotangent,
        branch_feed,
    )
    columns = [heads_grad[0], heads_grad[2], attn_grad_all, pre_grad, feed_grad_all]
    sums = [jnp.sum(value, axis=0, dtype=jnp.float32) for value in columns]
    vectors, modulation_all = gather_vectors(
        7, jnp.concatenate(sums + [silu_cond[0].astype(jnp.float32)]), rows
    )
    bias_total = jnp.sum(vectors, axis=0)
    offsets = [0]
    for value in sums:
        offsets.append(offsets[-1] + value.shape[0])
    bias_grads = [bias_total[offsets[i] : offsets[i + 1]] for i in range(5)]
    share = model_width // n_d
    cond_share = lax.dynamic_slice_in_dim(
        vectors[:, offsets[-1] :], lax.axis_index("dp") * share, share, 1
    )
    grad_modulate_weight = exact_left(cond_share, modulation_all)
    heads_share = inner_share[:, : 3 * local_width].reshape(share, 3, local_width)
    return (
        output,
        token_grad,
        grad_modulate_weight,
        jnp.sum(modulation_all, axis=0),
        jnp.swapaxes(heads_share, 0, 1),
        jnp.stack(bias_grads[:2]),
        inner_share[:, 3 * local_width :].T,
        bias_grads[2],
        first_share,
        bias_grads[3],
        second_share.T,
        bias_grads[4],
    )


def solution(mesh):
    in_specs = (
        P(("dp", "tensor"), None),
        P("dp", None),
        P(None, "tensor"),
        P("tensor"),
        P(None, None, "tensor"),
        P(None, "tensor"),
        P("tensor", None),
        P(),
        P(None, "tensor"),
        P("tensor"),
        P("tensor", None),
        P(),
        P(("dp", "tensor"), None),
    )
    out_specs = (
        P(("dp", "tensor"), None),
        P(("dp", "tensor"), None),
        P("dp", "tensor"),
        P("tensor"),
        P(None, "dp", "tensor"),
        P(None, "tensor"),
        P("tensor", "dp"),
        P(),
        P("dp", "tensor"),
        P("tensor"),
        P("tensor", "dp"),
        P(),
    )
    return jax.shard_map(local, mesh=mesh, in_specs=in_specs, out_specs=out_specs, check_vma=False)
```
